32 devices in a mesh: groups: 1, lon: 32 (over z, y, x, core).
Axes of the slice: x: 2, y: 2, z: 4, core: 2. Of those that a mesh axis runs over, the one named last changes fastest.
Arguments:
- tokens: bfloat16 [512, 32, 1536], P(('groups', 'lon')), may hold values from -40 to 40, as said below
- qkv: bfloat16 [3, 512, 32, 1536], P(None, ('groups', 'lon')), may hold values from -6 to 6
- bias_table: float32 [24, 225], replicated, may hold values from -3 to 3
- out_weight: bfloat16 [1536, 1536], replicated, may hold values from -0.15625 to 0.15625
- norm_gain: float32 [1536], replicated, may hold values from 0.25 to 1.75
- router: bfloat16 [1536, 32], replicated, may hold values from -0.15625 to 0.15625
- expert_ids: int32 [512, 32, 1], P(('groups', 'lon')), may hold values from 0 to 31; in each aligned block of 512 rows (0 to 511, 512 to 1023, ..., all dimensions but the last counted through in order) at most 32 rows name the same one
- slot_expert: int32 [32], replicated, may hold values from 0 to 31, each once
- up_weight: bfloat16 [32, 1536, 1024], P('lon'), may hold values from -0.15625 to 0.15625
- down_weight: bfloat16 [32, 1024, 1536], P('lon'), may hold values from -0.1875 to 0.1875
Outputs:
- blended: bfloat16 [512, 32, 1536], P(('groups', 'lon'))
The draws below stay inside these ranges and needn't reach their ends.
Inputs may be any that keep to these rules, and one draw needn't show every extreme that they name: tokens: entries of a normal or uniform law times token and feature scales. `expert_ids`: among the 512 tokens of one device (columns of one device, all latitude rows) at most 32 name the same expert. `slot_expert`: each expert stands in exactly one slot; slot s lives on device s of lon.
All inputs are finite; a program needn't handle non-finite values.
Results may differ from the reference program's by a relative error of at most 0.0051.
Values may be sent and summed in bfloat16 or wider, within the bound.
A program may use at most 128 MiB of HBM per device.

```python
import math
import jax
import jax.numpy as jnp
import numpy as np
from jax import lax

D = 1536
HEAD = 64
HEADS = 24
FF = 1024
WIN = 8
SHIFT = 4
LAT_ROWS = 32
EXPERTS = 32
NLON = 512
TOK_DEV = 512
CAP = 32
N_LON = 32


def draw_tokens(key, part):
    key = jax.random.fold_in(key, 11)
    first, second, third = jax.random.split(key, 3)
    shape = (NLON, LAT_ROWS, D)
    row_scale = jnp.exp(jax.random.uniform(second, (NLON, LAT_ROWS, 1), minval=math.log(0.4), maxval=math.log(4.0)))
    col_scale = jnp.exp(jax.random.uniform(third, (1, 1, D), minval=math.log(0.6), maxval=math.log(1.6)))
    base = jnp.clip(jax.random.normal(first, shape), -6.0, 6.0)
    return (base * row_scale * col_scale).astype(jnp.bfloat16)


def draw_qkv(key, part):
    key = jax.random.fold_in(key, 23)
    first = jax.random.fold_in(key, 0)
    shape = (3, NLON, LAT_ROWS, D)
    base = jnp.clip(jax.random.normal(first, shape), -6.0, 6.0)
    return base.astype(jnp.bfloat16)


def block_scale(rng, dims, pieces, low, high):
    loudness, own = 1.0, jax.random.fold_in(rng, 6)
    for position, blocks in pieces:
        steps = jnp.exp(jax.random.uniform(jax.random.fold_in(own, position), (blocks,), jnp.float32, low / len(pieces), high / len(pieces)))
        loudness = loudness * jnp.repeat(steps, dims[position] // blocks).reshape([-1 if axis == position else 1 for axis in range(len(dims))])
    return loudness


def deal_out(stream_key, own, number, rows, count, top, most, slope):
    order = jax.random.permutation(stream_key, count)
    packed, usual = shares(count, rows * top, most, slope, True), shares(count, rows * top, most, slope, False)
    places = jnp.arange(count)

    def named(sizes, rotation):
        used = int((sizes > 0).sum())
        fixed = max(1, used // 4)
        passed = fixed + (places - fixed + rotation * (used - fixed)) % max(1, count - fixed)
        return jnp.zeros((count,), jnp.int32).at[order[jnp.where(places < fixed, places, passed)]].set(jnp.asarray(sizes, jnp.int32))

    sizes = jnp.where(number % 4 == 0, named(packed, number // 4), named(usual, number - number // 4 - 1))
    mixed = jax.random.permutation(jax.random.fold_in(own, 3), count)
    source_of, receiver = mixed[0:count // 2 * 2:2], mixed[1:count // 2 * 2:2]
    room = jnp.minimum(sizes[source_of] - 1, most - sizes[receiver]) // 2
    room = jnp.where((source_of == order[0]) | (receiver == order[0]) | (sizes[receiver] == 0), 0, jnp.maximum(room, 0))
    passed = jax.random.randint(jax.random.fold_in(own, 4), (count // 2,), 0, 1 << 20) % (room + 1)
    sizes = sizes.at[source_of].add(-passed).at[receiver].add(passed)
    items = jnp.searchsorted(jnp.cumsum(sizes), jnp.arange(rows * top), side="right").astype(jnp.int32)
    listing = items.reshape(top, rows).T
    listing = listing[jax.random.permutation(jax.random.fold_in(own, 1), rows)]
    rotation = jax.random.randint(jax.random.fold_in(own, 2), (rows, 1), 0, top)
    return jnp.take_along_axis(listing, (jnp.arange(top)[None, :] + rotation) % top, axis=1)


def shares(count, total, most, slope, full):
    loads = [(1 << 20) // math.isqrt(grade ** slope) + 1 for grade in range(1, count + 1)]
    largest = most if full else min(most, max(-(-total // count), total * loads[0] // sum(loads)))
    least = 1 if total - largest >= count - 1 else 0
    counts, rest = [largest] + [least] * (count - 1), total - largest - least * (count - 1)
    while rest > 0:
        free = [i for i in range(1, count) if counts[i] < largest] or [i for i in range(1, count) if counts[i] < most]
        pool, remaining = sum([loads[i] for i in free]), rest
        for i in free:
            extra = min(most - counts[i], max(1, remaining * loads[i] // pool), rest)
            counts[i] = counts[i] + extra
            rest = rest - extra
    return np.array(counts)


def noise(stream_key, extent, deviation, bound, shards=(), held_as=jnp.bfloat16):
    drawn = jax.random.normal(stream_key, extent, jnp.float32) * deviation
    if len(shards) > 0:
        drawn = block_scale(stream_key, extent, shards, -0.22, 0.18) * drawn
    return jnp.clip(drawn, min=-bound, max=bound).astype(held_as)


def setup_inputs(seed: int = 0, part: int = 0) -> dict:
    seeds = jax.random.split(jax.random.key(seed), 11)
    part_keys = jax.random.split(jax.random.fold_in(seeds[10], part), 11)
    tokens = draw_tokens(jax.random.fold_in(jax.random.fold_in(seeds[10], part), 71), part)
    qkv = draw_qkv(jax.random.fold_in(jax.random.fold_in(seeds[10], part), 71), part)
    bias_table = noise(seeds[2], (HEADS, (2 * WIN - 1) * (2 * WIN - 1)), 1.0, 3.0, (), jnp.float32)
    out_weight = noise(seeds[3], (D, D), D ** -0.5, 0.15625)
    norm_gain = jnp.clip(1.0 + 0.15 * jax.random.normal(seeds[4], (D,), jnp.float32), 0.25, 1.75)
    router = noise(seeds[5], (D, EXPERTS), D ** -0.5, 0.15625)
    expert_ids_keys = jax.random.split(jax.random.fold_in(part_keys[6], 1), NLON * LAT_ROWS // TOK_DEV)
    expert_ids_turns = jax.random.permutation(jax.random.fold_in(part_keys[6], 3), NLON * LAT_ROWS // TOK_DEV)
    expert_ids = jax.vmap(lambda own, number: deal_out(jax.random.fold_in(part_keys[6], 2), own, number, TOK_DEV, EXPERTS, 1, CAP, 2))(expert_ids_keys, expert_ids_turns).reshape((NLON, LAT_ROWS, 1))
    slot_expert = jax.random.permutation(seeds[7], EXPERTS).astype(jnp.int32)
    up_weight = noise(seeds[8], (EXPERTS, D, FF), D ** -0.5, 0.15625, ((0, 32),))
    down_weight = noise(seeds[9], (EXPERTS, FF, D), FF ** -0.5, 0.1875, ((0, 32),))
    return dict(tokens=tokens, qkv=qkv, bias_table=bias_table, out_weight=out_weight, norm_gain=norm_gain, router=router, expert_ids=expert_ids, slot_expert=slot_expert, up_weight=up_weight, down_weight=down_weight)


def bias_index():
    lon_offset = np.arange(WIN * WIN) // WIN
    lat_offset = np.arange(WIN * WIN) % WIN
    along_lon = lon_offset[:, None] - lon_offset[None, :] + WIN - 1
    along_lat = lat_offset[:, None] - lat_offset[None, :] + WIN - 1
    return along_lon * (2 * WIN - 1) + along_lat

def region_labels(lat_count):
    rolled_rows = jnp.arange(lat_count)
    return jnp.where(rolled_rows < lat_count - WIN, 0, jnp.where(rolled_rows < lat_count - SHIFT, 1, 2)).astype(jnp.int32)

def to_windows(grid):
    lon_count, lat_count, features = grid.shape
    blocks = grid.reshape(lon_count // WIN, WIN, lat_count // WIN, WIN, features).transpose(0, 2, 1, 3, 4)
    return blocks.reshape(lon_count // WIN * (lat_count // WIN), WIN * WIN, features)

def from_windows(windows, lon_count, lat_count):
    features = windows.shape[-1]
    blocks = windows.reshape(lon_count // WIN, lat_count // WIN, WIN, WIN, features).transpose(0, 2, 1, 3, 4)
    return blocks.reshape(lon_count, lat_count, features)

def attend(queries, keys_win, values, labels, bias_table):
    win_count = queries.shape[0]
    head_count = queries.shape[-1] // HEAD
    query_heads = queries.astype(jnp.float32).reshape(win_count, WIN * WIN, head_count, HEAD)
    key_heads = keys_win.astype(jnp.float32).reshape(win_count, WIN * WIN, head_count, HEAD)
    value_heads = values.astype(jnp.float32).reshape(win_count, WIN * WIN, head_count, HEAD)
    scores = jnp.einsum('wqhd,wkhd->whqk', query_heads, key_heads) / math.sqrt(HEAD)
    scores = scores + bias_table[:, bias_index()][None]
    allowed = labels[:, :, None] == labels[:, None, :]
    scores = jnp.where(allowed[:, None], scores, -1000000000.0)
    highest = lax.optimization_barrier(jnp.max(scores, axis=-1, keepdims=True))
    weights = jnp.exp(scores - highest)
    weights_bf = (weights / lax.optimization_barrier(jnp.sum(weights, axis=-1, keepdims=True))).astype(jnp.bfloat16)
    attended = jnp.einsum('whqk,wkhd->wqhd', weights_bf.astype(jnp.float32), value_heads)
    return attended.reshape(win_count, WIN * WIN, head_count * HEAD).astype(jnp.bfloat16)

def reference(tokens, qkv, bias_table, out_weight, norm_gain, router, expert_ids, slot_expert, up_weight, down_weight):
    rolled = jnp.roll(qkv, (-SHIFT, -SHIFT), axis=(1, 2))
    label_grid = jnp.broadcast_to(region_labels(LAT_ROWS)[None, :, None], (NLON, LAT_ROWS, 1))
    labels = to_windows(label_grid)[:, :, 0]
    attended = attend(to_windows(rolled[0]), to_windows(rolled[1]), to_windows(rolled[2]), labels, bias_table)
    attended = jnp.roll(from_windows(attended, NLON, LAT_ROWS), (SHIFT, SHIFT), axis=(0, 1))
    projected = jnp.dot(attended.reshape(-1, D), out_weight, preferred_element_type=jnp.float32)
    resid = (tokens.reshape(-1, D).astype(jnp.float32) + projected).astype(jnp.bfloat16)
    resid_f = resid.astype(jnp.float32)
    scale = lax.rsqrt(lax.optimization_barrier(jnp.mean(resid_f * resid_f, axis=-1, keepdims=True)) + 1e-05)
    normed = (resid_f * scale * norm_gain[None, :]).astype(jnp.bfloat16)
    logits = jnp.dot(normed, router, preferred_element_type=jnp.float32)
    chosen = expert_ids.reshape(-1).astype(jnp.int32)
    expert_range = jnp.arange(EXPERTS).astype(jnp.int32)
    picked = lax.optimization_barrier(jnp.sum(jnp.where(chosen[:, None] == expert_range[None, :], logits, 0.0), axis=-1))
    gate = jax.nn.sigmoid(picked)
    slot_of = lax.optimization_barrier(jnp.sum(jnp.where(slot_expert[None, :] == expert_range[:, None], expert_range[None, :], 0), axis=1)).astype(jnp.int32)
    capacity = N_LON * CAP

    def run_expert(expert):
        members = jnp.nonzero(chosen == expert, size=capacity, fill_value=0)[0].astype(jnp.int32)
        valid = jnp.arange(capacity) < jnp.sum((chosen == expert).astype(jnp.int32))
        inputs_rows = jnp.where(valid[:, None], normed[members], jnp.zeros((), jnp.bfloat16))
        slot = slot_of[expert]
        up_slot = lax.dynamic_index_in_dim(up_weight, slot, 0, False)
        down_slot = lax.dynamic_index_in_dim(down_weight, slot, 0, False)
        hidden = jax.nn.gelu(jnp.dot(inputs_rows, up_slot, preferred_element_type=jnp.float32)).astype(jnp.bfloat16)
        outputs = jnp.dot(hidden, down_slot, preferred_element_type=jnp.float32).astype(jnp.bfloat16)
        return (members, jnp.where(valid[:, None], outputs.astype(jnp.float32), 0.0))
    members, outputs = lax.map(run_expert, expert_range)
    combined = jnp.zeros((NLON * LAT_ROWS, D), jnp.float32).at[members.reshape(-1)].add(outputs.reshape(-1, D))
    blended = resid_f + gate[:, None] * combined
    return blended.astype(jnp.bfloat16).reshape(NLON, LAT_ROWS, D)
```

```python
import functools

import jax
import jax.numpy as jnp
import numpy as np
from jax import lax
from jax.experimental import pallas as pl
from jax.experimental.pallas import tpu as pltpu
from jax.sharding import PartitionSpec as P

HEAD = 64
WIN = 8
SHIFT = 4
GROUP = 4
WIDE = GROUP * HEAD
F32 = jnp.float32
BF16 = jnp.bfloat16


def from_behind(value, axis, steps):
    count = lax.axis_size(axis)
    pairs = [(source, (source + steps) % count) for source in range(count)]
    return lax.ppermute(value, axis, pairs)


def bias_spread():
    side = 2 * WIN - 1
    spread = np.zeros((side * side, WIN, 128), np.float32)
    for row in range(WIN):
        for block in range(side):
            for col in range(WIN):
                entry = (side - 1 - block) * side + row - col + WIN - 1
                spread[entry, row, block * WIN + col] = 1.0
    return spread.reshape(side * side, WIN * 128)


def shift_up(grid):
    grid = grid.astype(F32)
    return jnp.concatenate([grid[:, SHIFT:], grid[:, :SHIFT]], axis=1)


def front_kernel(
    q_ref, k_ref, v_ref, prev_ref, next_ref, strip_ref, weight_ref, tokens_ref, gain_ref,
    router_ref, chosen_ref, resid_ref, normed_ref, gate_ref, total, rolled,
):
    step = pl.program_id(0)
    columns, lats = q_ref.shape[1], q_ref.shape[2]
    lat_windows = lats // WIN
    q = shift_up(q_ref[0]) * (1.0 / 8.0)
    k = shift_up(k_ref[0])
    v = shift_up(v_ref[0])
    prev_k, prev_v = shift_up(prev_ref[0]), shift_up(prev_ref[1])
    next_k, next_v = shift_up(next_ref[0]), shift_up(next_ref[1])

    heads = []
    for head in range(GROUP):
        strip = strip_ref[head]
        heads.append(
            jnp.concatenate(
                [strip[:, WIN * (WIN - 1 - a) : WIN * (WIN - 1 - a) + HEAD] for a in range(WIN)], axis=0
            )
        )
    bias = jnp.concatenate(heads, axis=1)

    lane_head = lax.broadcasted_iota(jnp.int32, (WIN * WIN, WIDE), 1) // HEAD
    ones = (
        lax.broadcasted_iota(jnp.int32, (WIDE, WIDE), 0) // HEAD
        == lax.broadcasted_iota(jnp.int32, (WIDE, WIDE), 1) // HEAD
    ).astype(BF16)

    def spread(block):
        return jnp.concatenate(
            [jnp.where(lane_head == head, block, jnp.zeros_like(block)) for head in range(GROUP)], axis=0
        )

    plans = [(0, SHIFT, SHIFT, jnp.concatenate([prev_k, k[:SHIFT]], 0), jnp.concatenate([prev_v, v[:SHIFT]], 0))]
    for first in range(SHIFT, columns - SHIFT, WIN):
        plans.append((first, WIN, 0, k[first : first + WIN], v[first : first + WIN]))
    last = columns - SHIFT
    plans.append((last, SHIFT, 0, jnp.concatenate([k[last:], next_k], 0), jnp.concatenate([v[last:], next_v], 0)))

    for first, width, a_from, keys, values in plans:
        rows = width * WIN
        bias_rows = bias[a_from * WIN : a_from * WIN + rows]
        row_lat = lax.broadcasted_iota(jnp.int32, (rows, WIDE), 0) % WIN
        lane = lax.broadcasted_iota(jnp.int32, (rows, WIDE), 1)
        allowed = (row_lat < SHIFT) == (lane % WIN < SHIFT)
        own = lane // HEAD
        for w in range(lat_windows):
            span = slice(w * WIN, (w + 1) * WIN)
            qw = q[first : first + width, span].reshape(rows, WIDE).astype(BF16)
            kw = keys[:, span].reshape(WIN * WIN, WIDE).astype(BF16)
            vw = values[:, span].reshape(WIN * WIN, WIDE).astype(BF16)
            scores = lax.dot_general(qw, spread(kw), (((1,), (1,)), ((), ())), preferred_element_type=F32)
            scores = scores + bias_rows
            if w == lat_windows - 1:
                scores = jnp.where(allowed, scores, -1000000000.0)
            highest = jnp.zeros_like(scores)
            for head in range(GROUP):
                top = jnp.max(scores[:, head * HEAD : (head + 1) * HEAD], axis=-1, keepdims=True)
                highest = jnp.where(own == head, top, highest)
            weights = jnp.exp(scores - highest).astype(BF16)
            mixed = jnp.dot(weights, spread(vw), preferred_element_type=F32)
            sums = jnp.dot(weights, ones, preferred_element_type=F32)
            rolled[first : first + width, span] = (mixed / sums).reshape(width, WIN, WIDE)

    back = rolled[...]
    attended = jnp.concatenate([back[:, lats - SHIFT :], back[:, : lats - SHIFT]], axis=1)
    attended = attended.reshape(columns * lats, WIDE).astype(BF16)
    part = jnp.dot(attended, weight_ref[...], preferred_element_type=F32)

    @pl.when(step == 0)
    def _():
        total[...] = part

    @pl.when(step > 0)
    def _():
        total[...] += part

    @pl.when(step == pl.num_programs(0) - 1)
    def _():
        resid = (tokens_ref[...].astype(F32) + total[...]).astype(BF16)
        resid_ref[...] = resid
        resid_f = resid.astype(F32)
        scale = lax.rsqrt(jnp.mean(resid_f * resid_f, axis=-1, keepdims=True) + 1e-05)
        normed = (resid_f * scale * gain_ref[...]).astype(BF16)
        normed_ref[...] = normed
        logits = jnp.dot(normed, router_ref[...], preferred_element_type=F32)
        expert = lax.broadcasted_iota(jnp.int32, logits.shape, 1)
        picked = jnp.sum(jnp.where(chosen_ref[...] == expert, logits, 0.0), axis=-1, keepdims=True)
        gate_ref[...] = jax.nn.sigmoid(picked)


def front(tokens, qkv, from_prev, from_next, strips, out_weight, norm_gain, router, chosen):
    _, columns, lats, features = qkv.shape
    count = columns * lats
    experts = router.shape[1]
    slab = lambda which: pl.BlockSpec((1, columns, lats, WIDE), lambda g: (which, 0, 0, g))
    rim = pl.BlockSpec((2, SHIFT, lats, WIDE), lambda g: (0, 0, 0, g))
    whole = lambda *shape: pl.BlockSpec(shape, lambda g: (0,) * len(shape))
    return pl.pallas_call(
        front_kernel,
        grid=(features // WIDE,),
        in_specs=[
            slab(0), slab(1), slab(2), rim, rim,
            pl.BlockSpec((GROUP, WIN, 128), lambda g: (g, 0, 0)),
            pl.BlockSpec((WIDE, features), lambda g: (g, 0)),
            whole(count, features), whole(1, features), whole(features, experts), whole(count, 1),
        ],
        out_specs=[whole(count, features), whole(count, features), whole(count, 1)],
        out_shape=[
            jax.ShapeDtypeStruct((count, features), BF16),
            jax.ShapeDtypeStruct((count, features), BF16),
            jax.ShapeDtypeStruct((count, 1), F32),
        ],
        scratch_shapes=[pltpu.VMEM((count, features), F32), pltpu.VMEM((columns, lats, WIDE), F32)],
        compiler_params=pltpu.CompilerParams(vmem_limit_bytes=56 * 1024 * 1024),
        name="front",
    )(
        qkv, qkv, qkv, from_prev, from_next, strips, out_weight, tokens.reshape(count, features),
        norm_gain[None, :], router, chosen,
    )


def expert_apply(rows_in, up_local, down_local):
    features = rows_in.shape[-1]
    flat_rows = rows_in.reshape(-1, features)
    hidden = jax.nn.gelu(jnp.dot(flat_rows, up_local, preferred_element_type=F32)).astype(BF16)
    result = jnp.dot(hidden, down_local, preferred_element_type=F32).astype(BF16)
    return result.reshape(rows_in.shape)


def local(
    tokens,
    qkv,
    bias_table,
    out_weight,
    norm_gain,
    router,
    expert_ids,
    slot_expert,
    up_weight,
    down_weight,
):
    columns, lat_count, features = tokens.shape
    token_count = columns * lat_count
    from_next = from_behind(qkv[1:, :SHIFT], "lon", -1)
    from_prev = from_behind(qkv[1:, columns - SHIFT :], "lon", 1)
    strips = jnp.dot(bias_table, bias_spread(), precision=lax.Precision.HIGHEST).reshape(-1, WIN, 128)
    resid, normed, gate = front(
        tokens, qkv, from_prev, from_next, strips, out_weight, norm_gain, router,
        expert_ids.reshape(token_count, 1),
    )
    peers = lax.axis_size("lon")
    experts = up_weight.shape[0] * peers
    capacity = 2 * token_count // experts
    chosen = expert_ids.reshape(-1)
    expert_range = jnp.arange(experts, dtype=jnp.int32)
    chosen_hot = chosen[:, None] == expert_range[None, :]
    slot_of = jnp.sum(
        jnp.where(slot_expert[None, :] == expert_range[:, None], expert_range[None, :], 0), axis=1
    )
    target = jnp.sum(jnp.where(chosen_hot, slot_of[None, :], 0), axis=1)
    target_hot = (target[:, None] == jnp.arange(peers, dtype=jnp.int32)[None, :]).astype(jnp.int32)
    earlier = jnp.cumsum(target_hot, axis=0) - target_hot
    position = target * capacity + jnp.sum(earlier * target_hot, axis=1)
    selector = (position[None, :] == jnp.arange(peers * capacity, dtype=jnp.int32)[:, None]).astype(BF16)
    outgoing = jnp.dot(selector, normed, preferred_element_type=F32).astype(BF16)
    outgoing = outgoing.reshape(peers, capacity, features)
    incoming = lax.all_to_all(outgoing, "lon", split_axis=0, concat_axis=0, tiled=True)
    answers = expert_apply(incoming, up_weight[0], down_weight[0])
    returned = lax.all_to_all(answers, "lon", split_axis=0, concat_axis=0, tiled=True)
    gathered = jnp.einsum(
        "st,sd->td", selector, returned.reshape(-1, features), preferred_element_type=F32
    )
    blended = resid.astype(F32) + gate * gathered
    return blended.astype(BF16).reshape(columns, lat_count, features)


def solution(mesh):
    in_specs = (
        P(("groups", "lon"), None, None),
        P(None, ("groups", "lon"), None, None),
        P(),
        P(),
        P(),
        P(),
        P(("groups", "lon"), None, None),
        P(),
        P("lon", None, None),
        P("lon", None, None),
    )
    out_specs = P(("groups", "lon"), None, None)
    return jax.shard_map(local, mesh=mesh, in_specs=in_specs, out_specs=out_specs, check_vma=False)
```

```python
import functools

import jax
import jax.numpy as jnp
import numpy as np
from jax import lax
from jax.experimental import pallas as pl
from jax.experimental.pallas import tpu as pltpu
from jax.sharding import PartitionSpec as P

HEAD = 64
WIN = 8
SHIFT = 4
GROUP = 4
WIDE = GROUP * HEAD
QUARTERS = 4
F32 = jnp.float32
BF16 = jnp.bfloat16


def from_behind(value, axis, steps):
    count = lax.axis_size(axis)
    pairs = [(source, (source + steps) % count) for source in range(count)]
    return lax.ppermute(value, axis, pairs)


def bias_spread():
    side = 2 * WIN - 1
    spread = np.zeros((side * side, WIN, 128), np.float32)
    for row in range(WIN):
        for block in range(side):
            for col in range(WIN):
                entry = (side - 1 - block) * side + row - col + WIN - 1
                spread[entry, row, block * WIN + col] = 1.0
    return spread.reshape(side * side, WIN * 128)


def shift_up(grid):
    grid = grid.astype(F32)
    return jnp.concatenate([grid[:, SHIFT:], grid[:, :SHIFT]], axis=1)


def front_kernel(
    q_ref, k_ref, v_ref, prev_ref, next_ref, strip_ref, weight_ref, tokens_ref, gain_ref,
    router_ref, chosen_ref, resid_ref, normed_ref, gate_ref, total, rolled,
):
    step = pl.program_id(0)
    columns, lats = q_ref.shape[1], q_ref.shape[2]
    lat_windows = lats // WIN
    q = shift_up(q_ref[0]) * (1.0 / 8.0)
    k = shift_up(k_ref[0])
    v = shift_up(v_ref[0])
    prev_k, prev_v = shift_up(prev_ref[0]), shift_up(prev_ref[1])
    next_k, next_v = shift_up(next_ref[0]), shift_up(next_ref[1])

    heads = []
    for head in range(GROUP):
        strip = strip_ref[head]
        heads.append(
            jnp.concatenate(
                [strip[:, WIN * (WIN - 1 - a) : WIN * (WIN - 1 - a) + HEAD] for a in range(WIN)], axis=0
            )
        )
    bias = jnp.concatenate(heads, axis=1)

    lane_head = lax.broadcasted_iota(jnp.int32, (WIN * WIN, WIDE), 1) // HEAD
    ones = (
        lax.broadcasted_iota(jnp.int32, (WIDE, WIDE), 0) // HEAD
        == lax.broadcasted_iota(jnp.int32, (WIDE, WIDE), 1) // HEAD
    ).astype(BF16)

    def spread(block):
        return jnp.concatenate(
            [jnp.where(lane_head == head, block, jnp.zeros_like(block)) for head in range(GROUP)], axis=0
        )

    plans = [(0, SHIFT, SHIFT, jnp.concatenate([prev_k, k[:SHIFT]], 0), jnp.concatenate([prev_v, v[:SHIFT]], 0))]
    for first in range(SHIFT, columns - SHIFT, WIN):
        plans.append((first, WIN, 0, k[first : first + WIN], v[first : first + WIN]))
    last = columns - SHIFT
    plans.append((last, SHIFT, 0, jnp.concatenate([k[last:], next_k], 0), jnp.concatenate([v[last:], next_v], 0)))

    for first, width, a_from, keys, values in plans:
        rows = width * WIN
        bias_rows = bias[a_from * WIN : a_from * WIN + rows]
        row_lat = lax.broadcasted_iota(jnp.int32, (rows, WIDE), 0) % WIN
        lane = lax.broadcasted_iota(jnp.int32, (rows, WIDE), 1)
        allowed = (row_lat < SHIFT) == (lane % WIN < SHIFT)
        own = lane // HEAD
        for w in range(lat_windows):
            span = slice(w * WIN, (w + 1) * WIN)
            qw = q[first : first + width, span].reshape(rows, WIDE).astype(BF16)
            kw = keys[:, span].reshape(WIN * WIN, WIDE).astype(BF16)
            vw = values[:, span].reshape(WIN * WIN, WIDE).astype(BF16)
            scores = lax.dot_general(qw, spread(kw), (((1,), (1,)), ((), ())), preferred_element_type=F32)
            scores = scores + bias_rows
            if w == lat_windows - 1:
                scores = jnp.where(allowed, scores, -1000000000.0)
            highest = jnp.zeros_like(scores)
            for head in range(GROUP):
                top = jnp.max(scores[:, head * HEAD : (head + 1) * HEAD], axis=-1, keepdims=True)
                highest = jnp.where(own == head, top, highest)
            weights = jnp.exp(scores - highest).astype(BF16)
            mixed = jnp.dot(weights, spread(vw), preferred_element_type=F32)
            sums = jnp.dot(weights, ones, preferred_element_type=F32)
            rolled[first : first + width, span] = (mixed / sums).reshape(width, WIN, WIDE)

    back = rolled[...]
    attended = jnp.concatenate([back[:, lats - SHIFT :], back[:, : lats - SHIFT]], axis=1)
    attended = attended.reshape(columns * lats, WIDE).astype(BF16)
    part = jnp.dot(attended, weight_ref[...], preferred_element_type=F32)

    @pl.when(step == 0)
    def _():
        total[...] = part

    @pl.when(step > 0)
    def _():
        total[...] += part

    @pl.when(step == pl.num_programs(0) - 1)
    def _():
        resid = (tokens_ref[...].astype(F32) + total[...]).astype(BF16)
        resid_ref[...] = resid
        resid_f = resid.astype(F32)
        scale = lax.rsqrt(jnp.mean(resid_f * resid_f, axis=-1, keepdims=True) + 1e-05)
        normed = (resid_f * scale * gain_ref[...]).astype(BF16)
        normed_ref[...] = normed
        logits = jnp.dot(normed, router_ref[...], preferred_element_type=F32)
        expert = lax.broadcasted_iota(jnp.int32, logits.shape, 1)
        picked = jnp.sum(jnp.where(chosen_ref[...] == expert, logits, 0.0), axis=-1, keepdims=True)
        gate_ref[...] = jax.nn.sigmoid(picked)


def front(tokens, qkv, from_prev, from_next, strips, out_weight, norm_gain, router, chosen):
    _, columns, lats, features = qkv.shape
    count = columns * lats
    experts = router.shape[1]
    slab = lambda which: pl.BlockSpec((1, columns, lats, WIDE), lambda g: (which, 0, 0, g))
    rim = pl.BlockSpec((2, SHIFT, lats, WIDE), lambda g: (0, 0, 0, g))
    whole = lambda *shape: pl.BlockSpec(shape, lambda g: (0,) * len(shape))
    return pl.pallas_call(
        front_kernel,
        grid=(features // WIDE,),
        in_specs=[
            slab(0), slab(1), slab(2), rim, rim,
            pl.BlockSpec((GROUP, WIN, 128), lambda g: (g, 0, 0)),
            pl.BlockSpec((WIDE, features), lambda g: (g, 0)),
            whole(count, features), whole(1, features), whole(features, experts), whole(count, 1),
        ],
        out_specs=[whole(count, features), whole(count, features), whole(count, 1)],
        out_shape=[
            jax.ShapeDtypeStruct((count, features), BF16),
            jax.ShapeDtypeStruct((count, features), BF16),
            jax.ShapeDtypeStruct((count, 1), F32),
        ],
        scratch_shapes=[pltpu.VMEM((count, features), F32), pltpu.VMEM((columns, lats, WIDE), F32)],
        compiler_params=pltpu.CompilerParams(vmem_limit_bytes=56 * 1024 * 1024),
        name="front",
    )(
        qkv, qkv, qkv, from_prev, from_next, strips, out_weight, tokens.reshape(count, features),
        norm_gain[None, :], router, chosen,
    )


def expert_kernel(
    peers, place_row_ref, place_col_ref, normed_ref, resid_ref, gate_ref, up_hbm, down_hbm, out_ref,
    outgoing, incoming, answers, returned, total, up, down, load_sem, send_sem, recv_sem, back_sem, home_sem,
):
    me = lax.axis_index("lon")
    size = peers // QUARTERS
    rows = outgoing.shape[0] // QUARTERS
    cap = rows // size
    count = normed_ref.shape[0]
    mine, inner = me // size, me % size

    def block(index):
        return pl.ds(pl.multiple_of(index * cap, cap), cap)

    def span(quarter):
        return pl.ds(pl.multiple_of(quarter * rows, rows), rows)

    def there(target):
        return pltpu.make_async_remote_copy(
            src_ref=outgoing.at[block(target)], dst_ref=incoming.at[block(me)],
            send_sem=send_sem.at[target], recv_sem=recv_sem.at[me],
            device_id={"lon": target}, device_id_type=pl.DeviceIdType.MESH,
        )

    def back(source):
        return pltpu.make_async_remote_copy(
            src_ref=answers.at[block(source)], dst_ref=returned.at[block(me)],
            send_sem=back_sem.at[source], recv_sem=home_sem.at[me],
            device_id={"lon": source}, device_id_type=pl.DeviceIdType.MESH,
        )

    def landed(buffer, sems, source):
        return pltpu.make_async_remote_copy(
            src_ref=buffer.at[block(source)], dst_ref=buffer.at[block(source)],
            send_sem=sems.at[source], recv_sem=sems.at[source],
            device_id={"lon": source}, device_id_type=pl.DeviceIdType.MESH,
        )

    barrier = pltpu.get_barrier_semaphore()

    @pl.loop(1, peers)
    def _(offset):
        pl.semaphore_signal(
            barrier, inc=1, device_id={"lon": lax.rem(me + offset, peers)}, device_id_type=pl.DeviceIdType.MESH
        )

    load_up = pltpu.make_async_copy(up_hbm.at[0], up, load_sem.at[0])
    load_down = pltpu.make_async_copy(down_hbm.at[0], down, load_sem.at[1])
    load_up.start()
    load_down.start()
    pl.semaphore_wait(barrier, peers - 1)

    @pl.loop(0, QUARTERS)
    def _(step):
        quarter = lax.rem(mine + step + 2, QUARTERS)
        slot = quarter * rows + lax.broadcasted_iota(jnp.int32, (rows, count), 0)
        pick = jnp.where(slot == place_row_ref[...], 1.0, 0.0).astype(BF16)
        outgoing[span(quarter), :] = jnp.dot(pick, normed_ref[...], preferred_element_type=F32).astype(BF16)

        @pl.loop(0, size)
        def _(offset):
            target = quarter * size + lax.rem(inner + offset, size)

            @pl.when(target != me)
            def _():
                there(target).start()

            @pl.when(target == me)
            def _():
                incoming[block(me), :] = outgoing[block(me), :]

    load_up.wait()
    load_down.wait()

    @pl.loop(0, QUARTERS)
    def _(step):
        quarter = lax.rem(mine + 2 * QUARTERS - step - 2, QUARTERS)

        @pl.loop(0, size)
        def _(offset):
            source = quarter * size + offset

            @pl.when(source != me)
            def _():
                landed(incoming, recv_sem, source).wait_recv()

        inputs = incoming[span(quarter), :]
        hidden = jax.nn.gelu(jnp.dot(inputs, up[...], preferred_element_type=F32)).astype(BF16)
        answers[span(quarter), :] = jnp.dot(hidden, down[...], preferred_element_type=F32).astype(BF16)

        @pl.loop(0, size)
        def _(offset):
            source = quarter * size + lax.rem(inner + size - offset, size)

            @pl.when(source != me)
            def _():
                back(source).start()

            @pl.when(source == me)
            def _():
                returned[block(me), :] = answers[block(me), :]

    total[...] = jnp.zeros_like(total)

    @pl.loop(0, QUARTERS)
    def _(step):
        quarter = lax.rem(mine + step + 2, QUARTERS)

        @pl.loop(0, size)
        def _(offset):
            source = quarter * size + offset

            @pl.when(source != me)
            def _():
                landed(returned, home_sem, source).wait_recv()

        slot = quarter * rows + lax.broadcasted_iota(jnp.int32, (count, rows), 1)
        pick = jnp.where(slot == place_col_ref[...], 1.0, 0.0).astype(BF16)
        total[...] += jnp.dot(pick, returned[span(quarter), :], preferred_element_type=F32)

    out_ref[...] = (resid_ref[...].astype(F32) + gate_ref[...] * total[...]).astype(BF16)

    @pl.loop(0, peers)
    def _(target):
        @pl.when(target != me)
        def _():
            there(target).wait_send()
            back(target).wait_send()


def expert_layer(position, normed, resid, gate, up_weight, down_weight, slots):
    count, features = normed.shape
    hidden = up_weight.shape[-1]
    peers = lax.axis_size("lon")
    vmem = pl.BlockSpec(memory_space=pltpu.VMEM)
    hbm = pl.BlockSpec(memory_space=pl.ANY)
    return pl.pallas_call(
        functools.partial(expert_kernel, peers),
        out_shape=jax.ShapeDtypeStruct((count, features), BF16),
        in_specs=[vmem] * 5 + [hbm] * 2,
        out_specs=vmem,
        scratch_shapes=[pltpu.VMEM((slots, features), BF16)] * 4
        + [
            pltpu.VMEM((count, features), F32),
            pltpu.VMEM((features, hidden), BF16),
            pltpu.VMEM((hidden, features), BF16),
            pltpu.SemaphoreType.DMA((2,)),
        ]
        + [pltpu.SemaphoreType.DMA((peers,))] * 4,
        compiler_params=pltpu.CompilerParams(
            collective_id=1, has_side_effects=True, vmem_limit_bytes=56 * 1024 * 1024
        ),
        name="experts",
    )(position[None, :], position[:, None], normed, resid, gate, up_weight, down_weight)


def local(
    tokens,
    qkv,
    bias_table,
    out_weight,
    norm_gain,
    router,
    expert_ids,
    slot_expert,
    up_weight,
    down_weight,
):
    columns, lat_count, features = tokens.shape
    token_count = columns * lat_count
    from_next = from_behind(qkv[1:, :SHIFT], "lon", -1)
    from_prev = from_behind(qkv[1:, columns - SHIFT :], "lon", 1)
    strips = jnp.dot(bias_table, bias_spread(), precision=lax.Precision.HIGHEST).reshape(-1, WIN, 128)
    resid, normed, gate = front(
        tokens, qkv, from_prev, from_next, strips, out_weight, norm_gain, router,
        expert_ids.reshape(token_count, 1),
    )
    peers = lax.axis_size("lon")
    experts = up_weight.shape[0] * peers
    capacity = 2 * token_count // experts
    chosen = expert_ids.reshape(-1)
    expert_range = jnp.arange(experts, dtype=jnp.int32)
    chosen_hot = chosen[:, None] == expert_range[None, :]
    slot_of = jnp.sum(
        jnp.where(slot_expert[None, :] == expert_range[:, None], expert_range[None, :], 0), axis=1
    )
    target = jnp.sum(jnp.where(chosen_hot, slot_of[None, :], 0), axis=1)
    target_hot = (target[:, None] == jnp.arange(peers, dtype=jnp.int32)[None, :]).astype(jnp.int32)
    earlier = jnp.cumsum(target_hot, axis=0) - target_hot
    position = target * capacity + jnp.sum(earlier * target_hot, axis=1)
    blended = expert_layer(position, normed, resid, gate, up_weight, down_weight, peers * capacity)
    return blended.reshape(columns, lat_count, features)


def solution(mesh):
    in_specs = (
        P(("groups", "lon"), None, None),
        P(None, ("groups", "lon"), None, None),
        P(),
        P(),
        P(),
        P(),
        P(("groups", "lon"), None, None),
        P(),
        P("lon", None, None),
        P("lon", None, None),
    )
    out_specs = P(("groups", "lon"), None, None)
    return jax.shard_map(local, mesh=mesh, in_specs=in_specs, out_specs=out_specs, check_vma=False)
```

```python
import functools

import jax
import jax.numpy as jnp
import numpy as np
from jax import lax
from jax.experimental import pallas as pl
from jax.experimental.pallas import tpu as pltpu
from jax.sharding import PartitionSpec as P

HEAD = 64
WIN = 8
SHIFT = 4
GROUP = 4
WIDE = GROUP * HEAD
QUARTERS = 4
F32 = jnp.float32
BF16 = jnp.bfloat16


def bias_spread():
    side = 2 * WIN - 1
    spread = np.zeros((side * side, WIN, 128), np.float32)
    for row in range(WIN):
        for block in range(side):
            for col in range(WIN):
                entry = (side - 1 - block) * side + row - col + WIN - 1
                spread[entry, row, block * WIN + col] = 1.0
    return spread.reshape(side * side, WIN * 128)


def shift_up(grid):
    grid = grid.astype(F32)
    return jnp.concatenate([grid[:, SHIFT:], grid[:, :SHIFT]], axis=1)


def front_kernel(
    qkv_hbm, q_ref, k_ref, v_ref, strip_ref, weight_ref, tokens_ref, gain_ref, router_ref, chosen_ref,
    slot_ref, resid_ref, normed_ref, gate_ref, place_col_ref, place_row_ref,
    prev_ref, next_ref, total, rolled, prev_send, prev_recv, next_send, next_recv,
):
    step = pl.program_id(0)
    columns, lats = q_ref.shape[1], q_ref.shape[2]
    groups = prev_ref.shape[0]
    group = lax.rem(step, groups)
    lat_windows = lats // WIN
    last = columns - SHIFT
    rim = SHIFT * lats
    me, peers = lax.axis_index("lon"), lax.axis_size("lon")
    right, left = lax.rem(me + 1, peers), lax.rem(me + peers - 1, peers)

    def up(index):
        return pltpu.make_async_remote_copy(
            src_ref=qkv_hbm.at[pl.ds(1, 2), pl.ds(last, SHIFT), :, pl.ds(pl.multiple_of(index * WIDE, WIDE), WIDE)],
            dst_ref=prev_ref.at[index], send_sem=prev_send.at[index], recv_sem=prev_recv.at[index],
            device_id={"lon": right}, device_id_type=pl.DeviceIdType.MESH,
        )

    def down(index):
        return pltpu.make_async_remote_copy(
            src_ref=qkv_hbm.at[pl.ds(1, 2), pl.ds(0, SHIFT), :, pl.ds(pl.multiple_of(index * WIDE, WIDE), WIDE)],
            dst_ref=next_ref.at[index], send_sem=next_send.at[index], recv_sem=next_recv.at[index],
            device_id={"lon": left}, device_id_type=pl.DeviceIdType.MESH,
        )

    @pl.when(step == 0)
    def _():
        barrier = pltpu.get_barrier_semaphore()
        for neighbour in (left, right):
            pl.semaphore_signal(
                barrier, inc=1, device_id={"lon": neighbour}, device_id_type=pl.DeviceIdType.MESH
            )
        pl.semaphore_wait(barrier, 2)

        @pl.loop(0, groups)
        def _(index):
            up(index).start()
            down(index).start()

        total[...] = tokens_ref[...].astype(F32)

    heads = []
    for head in range(GROUP):
        strip = strip_ref[head]
        heads.append(
            jnp.concatenate(
                [strip[:, WIN * (WIN - 1 - a) : WIN * (WIN - 1 - a) + HEAD] for a in range(WIN)], axis=0
            )
        )
    bias = jnp.concatenate(heads, axis=1)

    lane_head = lax.broadcasted_iota(jnp.int32, (WIN * WIN, WIDE), 1) // HEAD
    ones = jnp.where(
        lax.broadcasted_iota(jnp.int32, (WIDE, WIDE), 0) // HEAD
        == lax.broadcasted_iota(jnp.int32, (WIDE, WIDE), 1) // HEAD,
        1.0,
        0.0,
    ).astype(BF16)

    def spread(block):
        return jnp.concatenate(
            [jnp.where(lane_head == head, block, jnp.zeros_like(block)) for head in range(GROUP)], axis=0
        )

    def attend(first, width, a_from, keys, values):
        rows = width * WIN
        queries = shift_up(q_ref[0, first : first + width]) * (1.0 / 8.0)
        bias_rows = bias[a_from * WIN : a_from * WIN + rows]
        row_lat = lax.broadcasted_iota(jnp.int32, (rows, WIDE), 0) % WIN
        lane = lax.broadcasted_iota(jnp.int32, (rows, WIDE), 1)
        allowed = (row_lat < SHIFT) == (lane % WIN < SHIFT)
        own = lane // HEAD
        for w in range(lat_windows):
            span = slice(w * WIN, (w + 1) * WIN)
            qw = queries[:, span].reshape(rows, WIDE).astype(BF16)
            kw = keys[:, span].reshape(WIN * WIN, WIDE).astype(BF16)
            vw = values[:, span].reshape(WIN * WIN, WIDE).astype(BF16)
            scores = lax.dot_general(qw, spread(kw), (((1,), (1,)), ((), ())), preferred_element_type=F32)
            scores = scores + bias_rows
            if w == lat_windows - 1:
                scores = jnp.where(allowed, scores, -1000000000.0)
            highest = jnp.zeros_like(scores)
            for head in range(GROUP):
                top = jnp.max(scores[:, head * HEAD : (head + 1) * HEAD], axis=-1, keepdims=True)
                highest = jnp.where(own == head, top, highest)
            weights = jnp.exp(scores - highest).astype(BF16)
            mixed = jnp.dot(weights, spread(vw), preferred_element_type=F32)
            sums = jnp.dot(weights, ones, preferred_element_type=F32)
            rolled[first : first + width, span] = (mixed / sums).reshape(width, WIN, WIDE)

    def project(back):
        attended = jnp.concatenate([back[:, lats - SHIFT :], back[:, : lats - SHIFT]], axis=1)
        attended = attended.reshape(-1, WIDE).astype(BF16)
        return jnp.dot(attended, weight_ref[...], preferred_element_type=F32)

    @pl.when(step < groups)
    def _():
        for first in range(SHIFT, last, WIN):
            span = slice(first, first + WIN)
            attend(first, WIN, 0, shift_up(k_ref[0, span]), shift_up(v_ref[0, span]))
        total[rim : last * lats] += project(rolled[SHIFT:last])

    @pl.when(step >= groups)
    def _():
        up(group).wait_recv()
        down(group).wait_recv()
        pairs = [
            (0, SHIFT, lambda which, ref: jnp.concatenate([prev_ref[group, which], ref[0, :SHIFT]], 0)),
            (last, 0, lambda which, ref: jnp.concatenate([ref[0, last:], next_ref[group, which]], 0)),
        ]
        for first, a_from, joined in pairs:
            attend(first, SHIFT, a_from, shift_up(joined(0, k_ref)), shift_up(joined(1, v_ref)))
        part = project(jnp.concatenate([rolled[:SHIFT], rolled[last:]], 0))
        total[:rim] += part[:rim]
        total[last * lats :] += part[rim:]

    @pl.when(step == 1)
    def _():
        count, experts = chosen_ref.shape[0], slot_ref.shape[1]
        cap = 2 * count // experts
        hot = jnp.where(chosen_ref[...] == slot_ref[...], 1.0, 0.0)
        row = lax.broadcasted_iota(jnp.int32, (count, count), 0)
        col = lax.broadcasted_iota(jnp.int32, (count, count), 1)
        before = jnp.where(col < row, 1.0, 0.0).astype(BF16)
        earlier = jnp.dot(before, hot.astype(BF16), preferred_element_type=F32)
        base = (lax.broadcasted_iota(jnp.int32, hot.shape, 1) * cap).astype(F32)
        place = jnp.sum(hot * (base + earlier), axis=-1, keepdims=True)
        place_col_ref[...] = place.astype(jnp.int32)
        place_row_ref[...] = jnp.sum(jnp.where(row == col, place, 0.0), axis=0, keepdims=True).astype(jnp.int32)

    @pl.when(step == pl.num_programs(0) - 1)
    def _():
        resid = total[...].astype(BF16)
        resid_ref[...] = resid
        resid_f = resid.astype(F32)
        scale = lax.rsqrt(jnp.mean(resid_f * resid_f, axis=-1, keepdims=True) + 1e-05)
        normed = (resid_f * scale * gain_ref[...]).astype(BF16)
        normed_ref[...] = normed
        logits = lax.dot_general(normed, router_ref[...], (((1,), (1,)), ((), ())), preferred_element_type=F32)
        expert = lax.broadcasted_iota(jnp.int32, logits.shape, 1)
        picked = jnp.sum(jnp.where(chosen_ref[...] == expert, logits, 0.0), axis=-1, keepdims=True)
        gate_ref[...] = jax.nn.sigmoid(picked)

        @pl.loop(0, groups)
        def _(index):
            up(index).wait_send()
            down(index).wait_send()


def front(tokens, qkv, strips, out_weight, norm_gain, router, chosen, slot_expert):
    _, columns, lats, features = qkv.shape
    count = columns * lats
    experts = router.shape[1]
    groups = features // WIDE
    slab = lambda which: pl.BlockSpec((1, columns, lats, WIDE), lambda g: (which, 0, 0, g % groups))
    whole = lambda *shape: pl.BlockSpec(shape, lambda g: (0,) * len(shape))
    halo = pltpu.VMEM((groups, 2, SHIFT, lats, WIDE), BF16)
    return pl.pallas_call(
        front_kernel,
        grid=(2 * groups,),
        in_specs=[
            pl.BlockSpec(memory_space=pl.ANY), slab(0), slab(1), slab(2),
            pl.BlockSpec((GROUP, WIN, 128), lambda g: (g % groups, 0, 0)),
            pl.BlockSpec((WIDE, features), lambda g: (g % groups, 0)),
            whole(count, features), whole(1, features), whole(experts, features), whole(count, 1),
            whole(1, experts),
        ],
        out_specs=[
            whole(count, features), whole(count, features), whole(count, 1), whole(count, 1), whole(1, count),
        ],
        out_shape=[
            jax.ShapeDtypeStruct((count, features), BF16),
            jax.ShapeDtypeStruct((count, features), BF16),
            jax.ShapeDtypeStruct((count, 1), F32),
            jax.ShapeDtypeStruct((count, 1), jnp.int32),
            jax.ShapeDtypeStruct((1, count), jnp.int32),
        ],
        scratch_shapes=[
            halo, halo, pltpu.VMEM((count, features), F32), pltpu.VMEM((columns, lats, WIDE), F32),
        ]
        + [pltpu.SemaphoreType.DMA((groups,))] * 4,
        compiler_params=pltpu.CompilerParams(
            collective_id=0, has_side_effects=True, vmem_limit_bytes=56 * 1024 * 1024
        ),
        name="front",
    )(
        qkv, qkv, qkv, qkv, strips, out_weight, tokens.reshape(count, features),
        norm_gain[None, :], router.T, chosen, slot_expert[None, :],
    )


def ahead(step):
    return 2 + step - (step // 2) * (2 * step - 1)


def expert_kernel(
    peers, place_row_ref, place_col_ref, normed_ref, up_hbm, down_hbm, out_ref,
    outgoing, incoming, answers, returned, total, up, down, load_sem, send_sem, recv_sem, back_sem, home_sem,
):
    me = lax.axis_index("lon")
    size = peers // QUARTERS
    rows = outgoing.shape[0] // QUARTERS
    cap = rows // size
    count = normed_ref.shape[0]
    mine, inner = me // size, me % size

    def block(index):
        return pl.ds(pl.multiple_of(index * cap, cap), cap)

    def span(quarter):
        return pl.ds(pl.multiple_of(quarter * rows, rows), rows)

    def there(target):
        return pltpu.make_async_remote_copy(
            src_ref=outgoing.at[block(target)], dst_ref=incoming.at[block(me)],
            send_sem=send_sem.at[target], recv_sem=recv_sem.at[me],
            device_id={"lon": target}, device_id_type=pl.DeviceIdType.MESH,
        )

    def back(source):
        return pltpu.make_async_remote_copy(
            src_ref=answers.at[block(source)], dst_ref=returned.at[block(me)],
            send_sem=back_sem.at[source], recv_sem=home_sem.at[me],
            device_id={"lon": source}, device_id_type=pl.DeviceIdType.MESH,
        )

    def landed(buffer, sems, source):
        return pltpu.make_async_remote_copy(
            src_ref=buffer.at[block(source)], dst_ref=buffer.at[block(source)],
            send_sem=sems.at[source], recv_sem=sems.at[source],
            device_id={"lon": source}, device_id_type=pl.DeviceIdType.MESH,
        )

    barrier = pltpu.get_barrier_semaphore()

    @pl.loop(1, peers)
    def _(offset):
        pl.semaphore_signal(
            barrier, inc=1, device_id={"lon": lax.rem(me + offset, peers)}, device_id_type=pl.DeviceIdType.MESH
        )

    load_up = pltpu.make_async_copy(up_hbm.at[0], up, load_sem.at[0])
    load_down = pltpu.make_async_copy(down_hbm.at[0], down, load_sem.at[1])
    load_up.start()
    load_down.start()
    pl.semaphore_wait(barrier, peers - 1)

    @pl.loop(0, QUARTERS)
    def _(step):
        quarter = lax.rem(mine + ahead(step), QUARTERS)
        slot = quarter * rows + lax.broadcasted_iota(jnp.int32, (rows, count), 0)
        pick = jnp.where(slot == place_row_ref[...], 1.0, 0.0).astype(BF16)
        outgoing[span(quarter), :] = jnp.dot(pick, normed_ref[...], preferred_element_type=F32).astype(BF16)

        @pl.loop(0, size)
        def _(offset):
            target = quarter * size + lax.rem(inner + offset, size)

            @pl.when(target != me)
            def _():
                there(target).start()

            @pl.when(target == me)
            def _():
                incoming[block(me), :] = outgoing[block(me), :]

    load_up.wait()
    load_down.wait()

    @pl.loop(0, QUARTERS)
    def _(step):
        quarter = lax.rem(mine + QUARTERS - ahead(step), QUARTERS)

        @pl.loop(0, size)
        def _(offset):
            source = quarter * size + offset

            @pl.when(source != me)
            def _():
                landed(incoming, recv_sem, source).wait_recv()

        inputs = incoming[span(quarter), :]
        hidden = jax.nn.gelu(jnp.dot(inputs, up[...], preferred_element_type=F32)).astype(BF16)
        answers[span(quarter), :] = jnp.dot(hidden, down[...], preferred_element_type=F32).astype(BF16)

        @pl.loop(0, size)
        def _(offset):
            source = quarter * size + lax.rem(inner + size - offset, size)

            @pl.when(source != me)
            def _():
                back(source).start()

            @pl.when(source == me)
            def _():
                returned[block(me), :] = answers[block(me), :]

    total[...] = jnp.zeros_like(total)

    @pl.loop(0, QUARTERS)
    def _(step):
        quarter = lax.rem(mine + ahead(step), QUARTERS)

        @pl.loop(0, size)
        def _(offset):
            source = quarter * size + offset

            @pl.when(source != me)
            def _():
                landed(returned, home_sem, source).wait_recv()

        slot = quarter * rows + lax.broadcasted_iota(jnp.int32, (count, rows), 1)
        pick = jnp.where(slot == place_col_ref[...], 1.0, 0.0).astype(BF16)
        total[...] += jnp.dot(pick, returned[span(quarter), :], preferred_element_type=F32)

    out_ref[...] = total[...].astype(BF16)

    @pl.loop(0, peers)
    def _(target):
        @pl.when(target != me)
        def _():
            there(target).wait_send()
            back(target).wait_send()


def expert_layer(place_row, place_col, normed, up_weight, down_weight, slots):
    count, features = normed.shape
    hidden = up_weight.shape[-1]
    peers = lax.axis_size("lon")
    vmem = pl.BlockSpec(memory_space=pltpu.VMEM)
    hbm = pl.BlockSpec(memory_space=pl.ANY)
    return pl.pallas_call(
        functools.partial(expert_kernel, peers),
        out_shape=jax.ShapeDtypeStruct((count, features), BF16),
        in_specs=[vmem] * 3 + [hbm] * 2,
        out_specs=vmem,
        scratch_shapes=[pltpu.VMEM((slots, features), BF16)] * 4
        + [
            pltpu.VMEM((count, features), F32),
            pltpu.VMEM((features, hidden), BF16),
            pltpu.VMEM((hidden, features), BF16),
            pltpu.SemaphoreType.DMA((2,)),
        ]
        + [pltpu.SemaphoreType.DMA((peers,))] * 4,
        compiler_params=pltpu.CompilerParams(
            collective_id=1, has_side_effects=True, vmem_limit_bytes=56 * 1024 * 1024
        ),
        name="experts",
    )(place_row, place_col, normed, up_weight, down_weight)


def local(
    tokens,
    qkv,
    bias_table,
    out_weight,
    norm_gain,
    router,
    expert_ids,
    slot_expert,
    up_weight,
    down_weight,
):
    columns, lat_count, features = tokens.shape
    token_count = columns * lat_count
    strips = jnp.dot(bias_table, bias_spread(), precision=lax.Precision.HIGHEST).reshape(-1, WIN, 128)
    resid, normed, gate, place_col, place_row = front(
        tokens, qkv, strips, out_weight, norm_gain, router, expert_ids.reshape(token_count, 1), slot_expert
    )
    peers = lax.axis_size("lon")
    capacity = 2 * token_count // peers
    gathered = expert_layer(place_row, place_col, normed, up_weight, down_weight, peers * capacity)
    blended = resid.astype(F32) + gate * gathered.astype(F32)
    return blended.astype(BF16).reshape(columns, lat_count, features)


def solution(mesh):
    in_specs = (
        P(("groups", "lon"), None, None),
        P(None, ("groups", "lon"), None, None),
        P(),
        P(),
        P(),
        P(),
        P(("groups", "lon"), None, None),
        P(),
        P("lon", None, None),
        P("lon", None, None),
    )
    out_specs = P(("groups", "lon"), None, None)
    return jax.shard_map(local, mesh=mesh, in_specs=in_specs, out_specs=out_specs, check_vma=False)
```

```python
import functools

import jax
import jax.numpy as jnp
import numpy as np
from jax import lax
from jax.experimental import pallas as pl
from jax.experimental.pallas import tpu as pltpu
from jax.sharding import PartitionSpec as P

HEAD = 64
WIN = 8
SHIFT = 4
GROUP = 4
WIDE = GROUP * HEAD
QUARTERS = 4
F32 = jnp.float32
BF16 = jnp.bfloat16


def bias_spread():
    side = 2 * WIN - 1
    spread = np.zeros((side * side, WIN, 128), np.float32)
    for row in range(WIN):
        for block in range(side):
            for col in range(WIN):
                entry = (side - 1 - block) * side + row - col + WIN - 1
                spread[entry, row, block * WIN + col] = 1.0
    return spread.reshape(side * side, WIN * 128)


def shift_up(grid):
    grid = grid.astype(F32)
    return jnp.concatenate([grid[:, SHIFT:], grid[:, :SHIFT]], axis=1)


def front_kernel(
    qkv_hbm, q_ref, k_ref, v_ref, strip_ref, weight_ref, tokens_ref, gain_ref, router_ref, chosen_ref,
    slot_ref, resid_ref, normed_ref, gate_ref, place_col_ref, place_row_ref,
    prev_ref, next_ref, total, rolled, prev_send, prev_recv, next_send, next_recv,
):
    step = pl.program_id(0)
    columns, lats = q_ref.shape[1], q_ref.shape[2]
    groups = prev_ref.shape[0]
    group = lax.rem(step, groups)
    lat_windows = lats // WIN
    last = columns - SHIFT
    rim = SHIFT * lats
    me, peers = lax.axis_index("lon"), lax.axis_size("lon")
    right, left = lax.rem(me + 1, peers), lax.rem(me + peers - 1, peers)

    def up(index):
        return pltpu.make_async_remote_copy(
            src_ref=qkv_hbm.at[pl.ds(1, 2), pl.ds(last, SHIFT), :, pl.ds(pl.multiple_of(index * WIDE, WIDE), WIDE)],
            dst_ref=prev_ref.at[index], send_sem=prev_send.at[index], recv_sem=prev_recv.at[index],
            device_id={"lon": right}, device_id_type=pl.DeviceIdType.MESH,
        )

    def down(index):
        return pltpu.make_async_remote_copy(
            src_ref=qkv_hbm.at[pl.ds(1, 2), pl.ds(0, SHIFT), :, pl.ds(pl.multiple_of(index * WIDE, WIDE), WIDE)],
            dst_ref=next_ref.at[index], send_sem=next_send.at[index], recv_sem=next_recv.at[index],
            device_id={"lon": left}, device_id_type=pl.DeviceIdType.MESH,
        )

    @pl.when(step == 0)
    def _():
        barrier = pltpu.get_barrier_semaphore()
        for neighbour in (left, right):
            pl.semaphore_signal(
                barrier, inc=1, device_id={"lon": neighbour}, device_id_type=pl.DeviceIdType.MESH
            )
        pl.semaphore_wait(barrier, 2)

        up(0).start()
        down(0).start()
        total[...] = tokens_ref[...].astype(F32)

    @pl.when(step < groups - 1)
    def _():
        up(step + 1).start()
        down(step + 1).start()

    heads = []
    for head in range(GROUP):
        strip = strip_ref[head]
        heads.append(
            jnp.concatenate(
                [strip[:, WIN * (WIN - 1 - a) : WIN * (WIN - 1 - a) + HEAD] for a in range(WIN)], axis=0
            )
        )
    bias = jnp.concatenate(heads, axis=1)

    lane_head = lax.broadcasted_iota(jnp.int32, (WIN * WIN, WIDE), 1) // HEAD
    ones = jnp.where(
        lax.broadcasted_iota(jnp.int32, (WIDE, WIDE), 0) // HEAD
        == lax.broadcasted_iota(jnp.int32, (WIDE, WIDE), 1) // HEAD,
        1.0,
        0.0,
    ).astype(BF16)

    def spread(block):
        return jnp.concatenate(
            [jnp.where(lane_head == head, block, jnp.zeros_like(block)) for head in range(GROUP)], axis=0
        )

    def attend(first, width, a_from, keys, values):
        rows = width * WIN
        queries = shift_up(q_ref[0, first : first + width]) * (1.0 / 8.0)
        bias_rows = bias[a_from * WIN : a_from * WIN + rows]
        row_lat = lax.broadcasted_iota(jnp.int32, (rows, WIDE), 0) % WIN
        lane = lax.broadcasted_iota(jnp.int32, (rows, WIDE), 1)
        allowed = (row_lat < SHIFT) == (lane % WIN < SHIFT)
        own = lane // HEAD
        for w in range(lat_windows):
            span = slice(w * WIN, (w + 1) * WIN)
            qw = queries[:, span].reshape(rows, WIDE).astype(BF16)
            kw = keys[:, span].reshape(WIN * WIN, WIDE).astype(BF16)
            vw = values[:, span].reshape(WIN * WIN, WIDE).astype(BF16)
            scores = lax.dot_general(qw, spread(kw), (((1,), (1,)), ((), ())), preferred_element_type=F32)
            scores = scores + bias_rows
            if w == lat_windows - 1:
                scores = jnp.where(allowed, scores, -1000000000.0)
            highest = jnp.zeros_like(scores)
            for head in range(GROUP):
                top = jnp.max(scores[:, head * HEAD : (head + 1) * HEAD], axis=-1, keepdims=True)
                highest = jnp.where(own == head, top, highest)
            weights = jnp.exp(scores - highest).astype(BF16)
            mixed = jnp.dot(weights, spread(vw), preferred_element_type=F32)
            sums = jnp.dot(weights, ones, preferred_element_type=F32)
            rolled[first : first + width, span] = (mixed / sums).reshape(width, WIN, WIDE)

    def project(back):
        attended = jnp.concatenate([back[:, lats - SHIFT :], back[:, : lats - SHIFT]], axis=1)
        attended = attended.reshape(-1, WIDE).astype(BF16)
        return jnp.dot(attended, weight_ref[...], preferred_element_type=F32)

    @pl.when(step < groups)
    def _():
        for first in range(SHIFT, last, WIN):
            span = slice(first, first + WIN)
            attend(first, WIN, 0, shift_up(k_ref[0, span]), shift_up(v_ref[0, span]))
        total[rim : last * lats] += project(rolled[SHIFT:last])

    @pl.when(step >= groups)
    def _():
        up(group).wait_recv()
        down(group).wait_recv()
        pairs = [
            (0, SHIFT, lambda which, ref: jnp.concatenate([prev_ref[group, which], ref[0, :SHIFT]], 0)),
            (last, 0, lambda which, ref: jnp.concatenate([ref[0, last:], next_ref[group, which]], 0)),
        ]
        for first, a_from, joined in pairs:
            attend(first, SHIFT, a_from, shift_up(joined(0, k_ref)), shift_up(joined(1, v_ref)))
        part = project(jnp.concatenate([rolled[:SHIFT], rolled[last:]], 0))
        total[:rim] += part[:rim]
        total[last * lats :] += part[rim:]

    @pl.when(step == 1)
    def _():
        count, experts = total.shape[0], slot_ref.shape[1]
        cap = 2 * count // experts
        hot = jnp.where(chosen_ref[...].reshape(count, 1) == slot_ref[...], 1.0, 0.0)
        row = lax.broadcasted_iota(jnp.int32, (count, count), 0)
        col = lax.broadcasted_iota(jnp.int32, (count, count), 1)
        before = jnp.where(col < row, 1.0, 0.0).astype(BF16)
        earlier = jnp.dot(before, hot.astype(BF16), preferred_element_type=F32)
        base = (lax.broadcasted_iota(jnp.int32, hot.shape, 1) * cap).astype(F32)
        place = jnp.sum(hot * (base + earlier), axis=-1, keepdims=True)
        place_col_ref[...] = place.astype(jnp.int32)
        place_row_ref[...] = jnp.sum(jnp.where(row == col, place, 0.0), axis=0, keepdims=True).astype(jnp.int32)

    @pl.when(step == pl.num_programs(0) - 1)
    def _():
        resid = total[...].astype(BF16)
        resid_ref[...] = resid
        resid_f = resid.astype(F32)
        scale = lax.rsqrt(jnp.mean(resid_f * resid_f, axis=-1, keepdims=True) + 1e-05)
        normed = (resid_f * scale * gain_ref[...].reshape(1, -1)).astype(BF16)
        normed_ref[...] = normed
        logits = lax.dot_general(normed, router_ref[...], (((1,), (1,)), ((), ())), preferred_element_type=F32)
        expert = lax.broadcasted_iota(jnp.int32, logits.shape, 1)
        picked = jnp.sum(jnp.where(chosen_ref[...].reshape(total.shape[0], 1) == expert, logits, 0.0), axis=-1, keepdims=True)
        gate_ref[...] = jax.nn.sigmoid(picked)

        @pl.loop(0, groups)
        def _(index):
            up(index).wait_send()
            down(index).wait_send()


def front(tokens, qkv, strips, out_weight, norm_gain, router, chosen, slot_expert):
    _, columns, lats, features = qkv.shape
    count = columns * lats
    experts = router.shape[1]
    groups = features // WIDE
    slab = lambda which: pl.BlockSpec((1, columns, lats, WIDE), lambda g: (which, 0, 0, g % groups))
    whole = lambda *shape: pl.BlockSpec(shape, lambda g: (0,) * len(shape))
    halo = pltpu.VMEM((groups, 2, SHIFT, lats, WIDE), BF16)
    return pl.pallas_call(
        front_kernel,
        grid=(2 * groups,),
        in_specs=[
            pl.BlockSpec(memory_space=pl.ANY), slab(0), slab(1), slab(2),
            pl.BlockSpec((GROUP, WIN, 128), lambda g: (g % groups, 0, 0)),
            pl.BlockSpec((WIDE, features), lambda g: (g % groups, 0)),
            whole(count, features), whole(features), whole(experts, features), whole(columns, lats, 1),
            whole(1, experts),
        ],
        out_specs=[
            whole(count, features), whole(count, features), whole(count, 1), whole(count, 1), whole(1, count),
        ],
        out_shape=[
            jax.ShapeDtypeStruct((count, features), BF16),
            jax.ShapeDtypeStruct((count, features), BF16),
            jax.ShapeDtypeStruct((count, 1), F32),
            jax.ShapeDtypeStruct((count, 1), jnp.int32),
            jax.ShapeDtypeStruct((1, count), jnp.int32),
        ],
        scratch_shapes=[
            halo, halo, pltpu.VMEM((count, features), F32), pltpu.VMEM((columns, lats, WIDE), F32),
        ]
        + [pltpu.SemaphoreType.DMA((groups,))] * 4,
        compiler_params=pltpu.CompilerParams(
            collective_id=0, has_side_effects=True, vmem_limit_bytes=56 * 1024 * 1024
        ),
        name="front",
    )(
        qkv, qkv, qkv, qkv, strips, out_weight, tokens.reshape(count, features),
        norm_gain, router.T, chosen, slot_expert[None, :],
    )


def ahead(step):
    return 2 + step - (step // 2) * (2 * step - 1)


def expert_kernel(
    peers, place_row_ref, place_col_ref, normed_ref, resid_ref, gate_ref, up_hbm, down_hbm, out_ref,
    outgoing, incoming, answers, returned, total, up, down, load_sem, send_sem, recv_sem, back_sem, home_sem,
):
    me = lax.axis_index("lon")
    size = peers // QUARTERS
    rows = outgoing.shape[0] // QUARTERS
    cap = rows // size
    count = normed_ref.shape[0]
    mine, inner = me // size, me % size

    def block(index):
        return pl.ds(pl.multiple_of(index * cap, cap), cap)

    def span(quarter):
        return pl.ds(pl.multiple_of(quarter * rows, rows), rows)

    def there(target):
        return pltpu.make_async_remote_copy(
            src_ref=outgoing.at[block(target)], dst_ref=incoming.at[block(me)],
            send_sem=send_sem.at[target], recv_sem=recv_sem.at[me],
            device_id={"lon": target}, device_id_type=pl.DeviceIdType.MESH,
        )

    def back(source):
        return pltpu.make_async_remote_copy(
            src_ref=answers.at[block(source)], dst_ref=returned.at[block(me)],
            send_sem=back_sem.at[source], recv_sem=home_sem.at[me],
            device_id={"lon": source}, device_id_type=pl.DeviceIdType.MESH,
        )

    def landed(buffer, sems, source):
        return pltpu.make_async_remote_copy(
            src_ref=buffer.at[block(source)], dst_ref=buffer.at[block(source)],
            send_sem=sems.at[source], recv_sem=sems.at[source],
            device_id={"lon": source}, device_id_type=pl.DeviceIdType.MESH,
        )

    barrier = pltpu.get_barrier_semaphore()

    @pl.loop(1, peers)
    def _(offset):
        pl.semaphore_signal(
            barrier, inc=1, device_id={"lon": lax.rem(me + offset, peers)}, device_id_type=pl.DeviceIdType.MESH
        )

    load_up = pltpu.make_async_copy(up_hbm.at[0], up, load_sem.at[0])
    load_down = pltpu.make_async_copy(down_hbm.at[0], down, load_sem.at[1])
    load_up.start()
    load_down.start()
    pl.semaphore_wait(barrier, peers - 1)

    def dispatch(step):
        quarter = lax.rem(mine + ahead(step), QUARTERS)
        slot = quarter * rows + lax.broadcasted_iota(jnp.int32, (rows, count), 0)
        pick = jnp.where(slot == place_row_ref[...], 1.0, 0.0).astype(BF16)
        outgoing[span(quarter), :] = jnp.dot(pick, normed_ref[...], preferred_element_type=F32).astype(BF16)

        @pl.loop(0, size)
        def _(offset):
            target = quarter * size + lax.rem(inner + offset, size)

            @pl.when(target != me)
            def _():
                there(target).start()

            @pl.when(target == me)
            def _():
                incoming[block(me), :] = outgoing[block(me), :]

    @pl.loop(0, 2)
    def _(step):
        dispatch(step)

    load_up.wait()
    load_down.wait()

    @pl.loop(0, QUARTERS)
    def _(step):
        quarter = lax.rem(mine + QUARTERS - ahead(step), QUARTERS)

        @pl.loop(0, size)
        def _(offset):
            source = quarter * size + offset

            @pl.when(source != me)
            def _():
                landed(incoming, recv_sem, source).wait_recv()

        @pl.when(step < QUARTERS - 2)
        def _():
            dispatch(step + 2)

        inputs = incoming[span(quarter), :]
        hidden = jax.nn.gelu(jnp.dot(inputs, up[...], preferred_element_type=F32)).astype(BF16)
        answers[span(quarter), :] = jnp.dot(hidden, down[...], preferred_element_type=F32).astype(BF16)

        @pl.loop(0, size)
        def _(offset):
            source = quarter * size + lax.rem(inner + size - offset, size)

            @pl.when(source != me)
            def _():
                back(source).start()

            @pl.when(source == me)
            def _():
                returned[block(me), :] = answers[block(me), :]

    total[...] = jnp.zeros_like(total)

    @pl.loop(0, QUARTERS)
    def _(step):
        quarter = lax.rem(mine + ahead(step), QUARTERS)

        @pl.loop(0, size)
        def _(offset):
            source = quarter * size + offset

            @pl.when(source != me)
            def _():
                landed(returned, home_sem, source).wait_recv()

        slot = quarter * rows + lax.broadcasted_iota(jnp.int32, (count, rows), 1)
        pick = jnp.where(slot == place_col_ref[...], 1.0, 0.0).astype(BF16)
        total[...] += jnp.dot(pick, returned[span(quarter), :], preferred_element_type=F32)

    out_ref[...] = (resid_ref[...].astype(F32) + gate_ref[...] * total[...]).astype(BF16)

    @pl.loop(0, peers)
    def _(target):
        @pl.when(target != me)
        def _():
            there(target).wait_send()
            back(target).wait_send()


def expert_layer(place_row, place_col, normed, resid, gate, up_weight, down_weight, slots):
    count, features = normed.shape
    hidden = up_weight.shape[-1]
    peers = lax.axis_size("lon")
    vmem = pl.BlockSpec(memory_space=pltpu.VMEM)
    hbm = pl.BlockSpec(memory_space=pl.ANY)
    return pl.pallas_call(
        functools.partial(expert_kernel, peers),
        out_shape=jax.ShapeDtypeStruct((count, features), BF16),
        in_specs=[vmem] * 5 + [hbm] * 2,
        out_specs=vmem,
        scratch_shapes=[pltpu.VMEM((slots, features), BF16)] * 4
        + [
            pltpu.VMEM((count, features), F32),
            pltpu.VMEM((features, hidden), BF16),
            pltpu.VMEM((hidden, features), BF16),
            pltpu.SemaphoreType.DMA((2,)),
        ]
        + [pltpu.SemaphoreType.DMA((peers,))] * 4,
        compiler_params=pltpu.CompilerParams(
            collective_id=1, has_side_effects=True, vmem_limit_bytes=56 * 1024 * 1024
        ),
        name="experts",
    )(place_row, place_col, normed, resid, gate, up_weight, down_weight)


def local(
    tokens,
    qkv,
    bias_table,
    out_weight,
    norm_gain,
    router,
    expert_ids,
    slot_expert,
    up_weight,
    down_weight,
):
    columns, lat_count, features = tokens.shape
    token_count = columns * lat_count
    strips = jnp.dot(bias_table, bias_spread(), precision=lax.Precision.HIGHEST).reshape(-1, WIN, 128)
    resid, normed, gate, place_col, place_row = front(
        tokens, qkv, strips, out_weight, norm_gain, router, expert_ids, slot_expert
    )
    peers = lax.axis_size("lon")
    capacity = 2 * token_count // peers
    blended = expert_layer(place_row, place_col, normed, resid, gate, up_weight, down_weight, peers * capacity)
    return blended.reshape(columns, lat_count, features)


def solution(mesh):
    in_specs = (
        P(("groups", "lon"), None, None),
        P(None, ("groups", "lon"), None, None),
        P(),
        P(),
        P(),
        P(),
        P(("groups", "lon"), None, None),
        P(),
        P("lon", None, None),
        P("lon", None, None),
    )
    out_specs = P(("groups", "lon"), None, None)
    return jax.shard_map(local, mesh=mesh, in_specs=in_specs, out_specs=out_specs, check_vma=False)
```

```python
import functools

import jax
import jax.numpy as jnp
import numpy as np
from jax import lax
from jax.experimental import pallas as pl
from jax.experimental.pallas import tpu as pltpu
from jax.sharding import PartitionSpec as P

HEAD = 64
WIN = 8
SHIFT = 4
GROUP = 4
WIDE = GROUP * HEAD
QUARTERS = 4
F32 = jnp.float32
BF16 = jnp.bfloat16


def bias_spread():
    side = 2 * WIN - 1
    spread = np.zeros((side * side, WIN, 128), np.float32)
    for row in range(WIN):
        for block in range(side):
            for col in range(WIN):
                entry = (side - 1 - block) * side + row - col + WIN - 1
                spread[entry, row, block * WIN + col] = 1.0
    return spread.reshape(side * side, WIN * 128)


def shift_up(grid):
    grid = grid.astype(F32)
    return jnp.concatenate([grid[:, SHIFT:], grid[:, :SHIFT]], axis=1)


def front_kernel(
    qkv_hbm, q_ref, k_ref, v_ref, strip_ref, weight_ref, tokens_ref, gain_ref, router_ref, chosen_ref,
    slot_ref, resid_ref, normed_ref, gate_ref, place_col_ref, place_row_ref,
    prev_ref, next_ref, total, rolled, prev_send, prev_recv, next_send, next_recv,
):
    step = pl.program_id(0)
    columns, lats = q_ref.shape[1], q_ref.shape[2]
    groups = prev_ref.shape[0]
    group = lax.rem(step, groups)
    lat_windows = lats // WIN
    last = columns - SHIFT
    rim = SHIFT * lats
    me, peers = lax.axis_index("lon"), lax.axis_size("lon")
    right, left = lax.rem(me + 1, peers), lax.rem(me + peers - 1, peers)

    def up(index):
        return pltpu.make_async_remote_copy(
            src_ref=qkv_hbm.at[pl.ds(1, 2), pl.ds(last, SHIFT), :, pl.ds(pl.multiple_of(index * WIDE, WIDE), WIDE)],
            dst_ref=prev_ref.at[index], send_sem=prev_send.at[index], recv_sem=prev_recv.at[index],
            device_id={"lon": right}, device_id_type=pl.DeviceIdType.MESH,
        )

    def down(index):
        return pltpu.make_async_remote_copy(
            src_ref=qkv_hbm.at[pl.ds(1, 2), pl.ds(0, SHIFT), :, pl.ds(pl.multiple_of(index * WIDE, WIDE), WIDE)],
            dst_ref=next_ref.at[index], send_sem=next_send.at[index], recv_sem=next_recv.at[index],
            device_id={"lon": left}, device_id_type=pl.DeviceIdType.MESH,
        )

    @pl.when(step == 0)
    def _():
        barrier = pltpu.get_barrier_semaphore()
        for neighbour in (left, right):
            pl.semaphore_signal(
                barrier, inc=1, device_id={"lon": neighbour}, device_id_type=pl.DeviceIdType.MESH
            )
        pl.semaphore_wait(barrier, 2)

        up(0).start()
        down(0).start()
        total[...] = tokens_ref[...].astype(F32)

    @pl.when(step < groups - 1)
    def _():
        up(step + 1).start()
        down(step + 1).start()

    heads = []
    for head in range(GROUP):
        strip = strip_ref[head]
        heads.append(
            jnp.concatenate(
                [strip[:, WIN * (WIN - 1 - a) : WIN * (WIN - 1 - a) + HEAD] for a in range(WIN)], axis=0
            )
        )
    bias = jnp.concatenate(heads, axis=1)

    lane_head = lax.broadcasted_iota(jnp.int32, (WIN * WIN, WIDE), 1) // HEAD
    ones = jnp.where(
        lax.broadcasted_iota(jnp.int32, (WIDE, WIDE), 0) // HEAD
        == lax.broadcasted_iota(jnp.int32, (WIDE, WIDE), 1) // HEAD,
        1.0,
        0.0,
    ).astype(BF16)

    def spread(block):
        return jnp.concatenate(
            [jnp.where(lane_head == head, block, jnp.zeros_like(block)) for head in range(GROUP)], axis=0
        )

    def attend(first, width, a_from, keys, values):
        rows = width * WIN
        queries = shift_up(q_ref[0, first : first + width]) * (1.0 / 8.0)
        bias_rows = bias[a_from * WIN : a_from * WIN + rows]
        row_lat = lax.broadcasted_iota(jnp.int32, (rows, WIDE), 0) % WIN
        lane = lax.broadcasted_iota(jnp.int32, (rows, WIDE), 1)
        allowed = (row_lat < SHIFT) == (lane % WIN < SHIFT)
        own = lane // HEAD
        for w in range(lat_windows):
            span = slice(w * WIN, (w + 1) * WIN)
            qw = queries[:, span].reshape(rows, WIDE).astype(BF16)
            kw = keys[:, span].reshape(WIN * WIN, WIDE).astype(BF16)
            vw = values[:, span].reshape(WIN * WIN, WIDE).astype(BF16)
            scores = lax.dot_general(qw, spread(kw), (((1,), (1,)), ((), ())), preferred_element_type=F32)
            scores = scores + bias_rows
            if w == lat_windows - 1:
                scores = jnp.where(allowed, scores, -1000000000.0)
            highest = jnp.zeros_like(scores)
            for head in range(GROUP):
                top = jnp.max(scores[:, head * HEAD : (head + 1) * HEAD], axis=-1, keepdims=True)
                highest = jnp.where(own == head, top, highest)
            weights = jnp.exp(scores - highest).astype(BF16)
            mixed = jnp.dot(weights, spread(vw), preferred_element_type=F32)
            sums = jnp.dot(weights, ones, preferred_element_type=F32)
            rolled[first : first + width, span] = (mixed / sums).reshape(width, WIN, WIDE)

    def project(back):
        attended = jnp.concatenate([back[:, lats - SHIFT :], back[:, : lats - SHIFT]], axis=1)
        attended = attended.reshape(-1, WIDE).astype(BF16)
        return jnp.dot(attended, weight_ref[...], preferred_element_type=F32)

    @pl.when(step < groups)
    def _():
        for first in range(SHIFT, last, WIN):
            span = slice(first, first + WIN)
            attend(first, WIN, 0, shift_up(k_ref[0, span]), shift_up(v_ref[0, span]))
        total[rim : last * lats] += project(rolled[SHIFT:last])

    @pl.when(step >= groups)
    def _():
        up(group).wait_recv()
        down(group).wait_recv()
        pairs = [
            (0, SHIFT, lambda which, ref: jnp.concatenate([prev_ref[group, which], ref[0, :SHIFT]], 0)),
            (last, 0, lambda which, ref: jnp.concatenate([ref[0, last:], next_ref[group, which]], 0)),
        ]
        for first, a_from, joined in pairs:
            attend(first, SHIFT, a_from, shift_up(joined(0, k_ref)), shift_up(joined(1, v_ref)))
        part = project(jnp.concatenate([rolled[:SHIFT], rolled[last:]], 0))
        total[:rim] += part[:rim]
        total[last * lats :] += part[rim:]

    @pl.when(step == 1)
    def _():
        count, experts = total.shape[0], slot_ref.shape[1]
        cap = 2 * count // experts
        hot = jnp.where(chosen_ref[...].reshape(count, 1) == slot_ref[...], 1.0, 0.0)
        row = lax.broadcasted_iota(jnp.int32, (count, count), 0)
        col = lax.broadcasted_iota(jnp.int32, (count, count), 1)
        before = jnp.where(col < row, 1.0, 0.0).astype(BF16)
        earlier = jnp.dot(before, hot.astype(BF16), preferred_element_type=F32)
        base = (lax.broadcasted_iota(jnp.int32, hot.shape, 1) * cap).astype(F32)
        place = jnp.sum(hot * (base + earlier), axis=-1, keepdims=True)
        place_col_ref[...] = place.astype(jnp.int32)
        place_row_ref[...] = jnp.sum(jnp.where(row == col, place, 0.0), axis=0, keepdims=True).astype(jnp.int32)

    @pl.when(step == pl.num_programs(0) - 1)
    def _():
        resid = total[...].astype(BF16)
        resid_ref[...] = resid
        resid_f = resid.astype(F32)
        scale = lax.rsqrt(jnp.mean(resid_f * resid_f, axis=-1, keepdims=True) + 1e-05)
        normed = (resid_f * scale * gain_ref[...].reshape(1, -1)).astype(BF16)
        normed_ref[...] = normed
        logits = lax.dot_general(normed, router_ref[...], (((1,), (1,)), ((), ())), preferred_element_type=F32)
        expert = lax.broadcasted_iota(jnp.int32, logits.shape, 1)
        picked = jnp.sum(jnp.where(chosen_ref[...].reshape(total.shape[0], 1) == expert, logits, 0.0), axis=-1, keepdims=True)
        gate_ref[...] = jax.nn.sigmoid(picked)

        @pl.loop(0, groups)
        def _(index):
            up(index).wait_send()
            down(index).wait_send()


def front(tokens, qkv, strips, out_weight, norm_gain, router, chosen, slot_expert):
    _, columns, lats, features = qkv.shape
    count = columns * lats
    experts = router.shape[1]
    groups = features // WIDE
    slab = lambda which: pl.BlockSpec((1, columns, lats, WIDE), lambda g: (which, 0, 0, g % groups))
    whole = lambda *shape: pl.BlockSpec(shape, lambda g: (0,) * len(shape))
    halo = pltpu.VMEM((groups, 2, SHIFT, lats, WIDE), BF16)
    return pl.pallas_call(
        front_kernel,
        grid=(2 * groups,),
        in_specs=[
            pl.BlockSpec(memory_space=pl.ANY), slab(0), slab(1), slab(2),
            pl.BlockSpec((GROUP, WIN, 128), lambda g: (g % groups, 0, 0)),
            pl.BlockSpec((WIDE, features), lambda g: (g % groups, 0)),
            whole(count, features), whole(features), whole(experts, features), whole(columns, lats, 1),
            whole(1, experts),
        ],
        out_specs=[
            whole(count, features), whole(count, features), whole(count, 1), whole(count, 1), whole(1, count),
        ],
        out_shape=[
            jax.ShapeDtypeStruct((count, features), BF16),
            jax.ShapeDtypeStruct((count, features), BF16),
            jax.ShapeDtypeStruct((count, 1), F32),
            jax.ShapeDtypeStruct((count, 1), jnp.int32),
            jax.ShapeDtypeStruct((1, count), jnp.int32),
        ],
        scratch_shapes=[
            halo, halo, pltpu.VMEM((count, features), F32), pltpu.VMEM((columns, lats, WIDE), F32),
        ]
        + [pltpu.SemaphoreType.DMA((groups,))] * 4,
        compiler_params=pltpu.CompilerParams(
            collective_id=0, has_side_effects=True, vmem_limit_bytes=56 * 1024 * 1024
        ),
        name="front",
    )(
        qkv, qkv, qkv, qkv, strips, out_weight, tokens.reshape(count, features),
        norm_gain, router.T, chosen, slot_expert[None, :],
    )


def ahead(step):
    return 2 + step - (step // 2) * (2 * step - 1)


def expert_kernel(
    peers, place_row_ref, place_col_ref, normed_ref, resid_ref, gate_ref, up_hbm, down_hbm, out_ref,
    outgoing, incoming, answers, returned, total, up, down, load_sem, send_sem, recv_sem, back_sem, home_sem,
):
    me = lax.axis_index("lon")
    size = peers // QUARTERS
    rows = outgoing.shape[0] // QUARTERS
    cap = rows // size
    count = normed_ref.shape[0]
    mine, inner = me // size, me % size

    def block(index):
        return pl.ds(pl.multiple_of(index * cap, cap), cap)

    def span(quarter):
        return pl.ds(pl.multiple_of(quarter * rows, rows), rows)

    def there(target):
        return pltpu.make_async_remote_copy(
            src_ref=outgoing.at[block(target)], dst_ref=incoming.at[block(me)],
            send_sem=send_sem.at[target], recv_sem=recv_sem.at[me],
            device_id={"lon": target}, device_id_type=pl.DeviceIdType.MESH,
        )

    def back(source):
        return pltpu.make_async_remote_copy(
            src_ref=answers.at[block(source)], dst_ref=returned.at[block(me)],
            send_sem=back_sem.at[source], recv_sem=home_sem.at[me],
            device_id={"lon": source}, device_id_type=pl.DeviceIdType.MESH,
        )

    def landed(buffer, sems, source):
        return pltpu.make_async_remote_copy(
            src_ref=buffer.at[block(source)], dst_ref=buffer.at[block(source)],
            send_sem=sems.at[source], recv_sem=sems.at[source],
            device_id={"lon": source}, device_id_type=pl.DeviceIdType.MESH,
        )

    barrier = pltpu.get_barrier_semaphore()

    @pl.loop(1, peers)
    def _(offset):
        pl.semaphore_signal(
            barrier, inc=1, device_id={"lon": lax.rem(me + offset, peers)}, device_id_type=pl.DeviceIdType.MESH
        )

    load_up = pltpu.make_async_copy(up_hbm.at[0], up, load_sem.at[0])
    load_down = pltpu.make_async_copy(down_hbm.at[0], down, load_sem.at[1])
    load_up.start()
    load_down.start()
    pl.semaphore_wait(barrier, peers - 1)

    def dispatch(step):
        quarter = lax.rem(mine + ahead(step), QUARTERS)
        slot = quarter * rows + lax.broadcasted_iota(jnp.int32, (rows, count), 0)
        pick = jnp.where(slot == place_row_ref[...], 1.0, 0.0).astype(BF16)
        outgoing[span(quarter), :] = jnp.dot(pick, normed_ref[...], preferred_element_type=F32).astype(BF16)

        @pl.loop(0, size)
        def _(offset):
            target = quarter * size + lax.rem(inner + offset, size)

            @pl.when(target != me)
            def _():
                there(target).start()

            @pl.when(target == me)
            def _():
                incoming[block(me), :] = outgoing[block(me), :]

    @pl.loop(0, QUARTERS - 1)
    def _(step):
        dispatch(step)

    load_up.wait()
    load_down.wait()

    @pl.loop(0, QUARTERS)
    def _(step):
        quarter = lax.rem(mine + QUARTERS - ahead(step), QUARTERS)

        @pl.loop(0, size)
        def _(offset):
            source = quarter * size + offset

            @pl.when(source != me)
            def _():
                landed(incoming, recv_sem, source).wait_recv()

        @pl.when(step == 0)
        def _():
            dispatch(QUARTERS - 1)

        inputs = incoming[span(quarter), :]
        hidden = jax.nn.gelu(jnp.dot(inputs, up[...], preferred_element_type=F32)).astype(BF16)
        answers[span(quarter), :] = jnp.dot(hidden, down[...], preferred_element_type=F32).astype(BF16)

        @pl.loop(0, size)
        def _(offset):
            source = quarter * size + lax.rem(inner + size - offset, size)

            @pl.when(source != me)
            def _():
                back(source).start()

            @pl.when(source == me)
            def _():
                returned[block(me), :] = answers[block(me), :]

    total[...] = jnp.zeros_like(total)

    @pl.loop(0, QUARTERS)
    def _(step):
        quarter = lax.rem(mine + ahead(step), QUARTERS)

        @pl.loop(0, size)
        def _(offset):
            source = quarter * size + offset

            @pl.when(source != me)
            def _():
                landed(returned, home_sem, source).wait_recv()

        slot = quarter * rows + lax.broadcasted_iota(jnp.int32, (count, rows), 1)
        pick = jnp.where(slot == place_col_ref[...], 1.0, 0.0).astype(BF16)
        total[...] += jnp.dot(pick, returned[span(quarter), :], preferred_element_type=F32)

    out_ref[...] = (resid_ref[...].astype(F32) + gate_ref[...] * total[...]).astype(BF16)

    @pl.loop(0, peers)
    def _(target):
        @pl.when(target != me)
        def _():
            there(target).wait_send()
            back(target).wait_send()


def expert_layer(place_row, place_col, normed, resid, gate, up_weight, down_weight, slots):
    count, features = normed.shape
    hidden = up_weight.shape[-1]
    peers = lax.axis_size("lon")
    vmem = pl.BlockSpec(memory_space=pltpu.VMEM)
    hbm = pl.BlockSpec(memory_space=pl.ANY)
    return pl.pallas_call(
        functools.partial(expert_kernel, peers),
        out_shape=jax.ShapeDtypeStruct((count, features), BF16),
        in_specs=[vmem] * 5 + [hbm] * 2,
        out_specs=vmem,
        scratch_shapes=[pltpu.VMEM((slots, features), BF16)] * 4
        + [
            pltpu.VMEM((count, features), F32),
            pltpu.VMEM((features, hidden), BF16),
            pltpu.VMEM((hidden, features), BF16),
            pltpu.SemaphoreType.DMA((2,)),
        ]
        + [pltpu.SemaphoreType.DMA((peers,))] * 4,
        compiler_params=pltpu.CompilerParams(
            collective_id=1, has_side_effects=True, vmem_limit_bytes=56 * 1024 * 1024
        ),
        name="experts",
    )(place_row, place_col, normed, resid, gate, up_weight, down_weight)


def local(
    tokens,
    qkv,
    bias_table,
    out_weight,
    norm_gain,
    router,
    expert_ids,
    slot_expert,
    up_weight,
    down_weight,
):
    columns, lat_count, features = tokens.shape
    token_count = columns * lat_count
    strips = jnp.dot(bias_table, bias_spread(), precision=lax.Precision.HIGHEST).reshape(-1, WIN, 128)
    resid, normed, gate, place_col, place_row = front(
        tokens, qkv, strips, out_weight, norm_gain, router, expert_ids, slot_expert
    )
    peers = lax.axis_size("lon")
    capacity = 2 * token_count // peers
    blended = expert_layer(place_row, place_col, normed, resid, gate, up_weight, down_weight, peers * capacity)
    return blended.reshape(columns, lat_count, features)


def solution(mesh):
    in_specs = (
        P(("groups", "lon"), None, None),
        P(None, ("groups", "lon"), None, None),
        P(),
        P(),
        P(),
        P(),
        P(("groups", "lon"), None, None),
        P(),
        P("lon", None, None),
        P("lon", None, None),
    )
    out_specs = P(("groups", "lon"), None, None)
    return jax.shard_map(local, mesh=mesh, in_specs=in_specs, out_specs=out_specs, check_vma=False)
```
